1024 devices in a mesh: fsdp: 128 (over z, y, x_hi), tp: 8 (over x_lo, core).
Axes of the slice: x: 8 (x_hi: 2, x_lo: 4; x = x_hi * 4 + x_lo), y: 8, z: 8, core: 2. Of those that a mesh axis runs over, the one named last changes fastest.
Arguments:
- hidden: bfloat16 [2, 9216, 16384], P(None, 'fsdp', 'tp'), may hold values from -6 to 6
- queries: bfloat16 [2, 9216, 16384], P(None, 'fsdp', 'tp'), may hold values from -256 to 256
- cache_keys: bfloat16 [9216, 32, 1024], P('fsdp', None, 'tp'), may hold values from -6 to 6
- cache_values: bfloat16 [9216, 32, 1024], P('fsdp', None, 'tp'), may hold values from -6 to 6
- new_values: bfloat16 [2, 9216, 1024], P(None, 'fsdp', 'tp'), may hold values from -6 to 6
- lengths: int32 [9216], P('fsdp'), may hold values from 2 to 32, as said below
- base_weight: bfloat16 [16384, 1024], P(None, 'tp'), may hold values from -0.046875 to 0.046875
- delta_values: bfloat16 [16384, 1024], P(('fsdp', 'tp')), may hold values from -4 to 4
- delta_scales: bfloat16 [128, 8], P('fsdp', 'tp'), may hold values from 0.0019989014 to 0.019897461
- block_order: int32 [128], replicated, may hold values from 0 to 127, each once
Outputs:
- attended: bfloat16 [2, 9216, 16384], P(None, 'fsdp', 'tp')
- new_keys: bfloat16 [2, 9216, 1024], P(None, 'fsdp', 'tp')
The draws below stay inside these ranges and needn't reach their ends.
Inputs may be any that keep to these rules, and one draw needn't show every extreme that they name: `lengths`: every row has at least two valid cached positions; some row holds 32. `block_order`: A permutation of the block rows.
All inputs are finite; a program needn't handle non-finite values.
Results may differ from the reference program's by a relative error of at most 0.0056.
Values may be sent and summed in bfloat16 or wider, within the bound.
A program may use at most 64 MiB of HBM per device.

```python
import math
import jax
import jax.numpy as jnp
from jax import lax

D = 16384
HD = 128
KVH = 8
QH = 128
BLK = 128
STEPS = 2
CAP = 32
RTOT = 9216
KVD = 1024
NBR = 128


def shared_keys(key):
    return jnp.clip(jax.random.normal(key, (RTOT, CAP, KVH * HD), jnp.float32), -6.0, 6.0)


def draw_cache_keys(key, part):
    keys_drawn = shared_keys(key)
    return keys_drawn.astype(jnp.bfloat16)


def draw_queries(key, part):
    key = jax.random.fold_in(key, 12)
    noise = jnp.clip(jax.random.normal(key, (STEPS, RTOT, QH * HD), jnp.float32), -6.0, 6.0)
    return noise.astype(jnp.bfloat16)


def draw_lengths(key, part):
    key = jax.random.fold_in(key, 13)
    drawn = jax.random.randint(key, (RTOT,), 2, CAP + 1, jnp.int32)
    return drawn.at[0].set(CAP)


def steps_of(rng, shape, shards, least, top_value):
    factor_of = 1.0
    for position, shards_of in shards:
        steps = jax.random.uniform(jax.random.fold_in(jax.random.fold_in(rng, 6), position), (shards_of,), jnp.float32, least / len(shards), top_value / len(shards))
        factor_of = factor_of * jnp.repeat(jnp.exp(steps), shape[position] // shards_of).reshape((-1,) + (1,) * (len(shape) - 1 - position))
    return factor_of


def gaussian(rng, dims, spread, limit, shards=(), held_as=jnp.bfloat16):
    values = jax.random.normal(rng, dims, jnp.float32) * spread
    if len(shards) > 0:
        values = steps_of(rng, dims, shards, -0.22, 0.18) * values
    return jnp.clip(values, min=-limit, max=limit).astype(held_as)


def setup_inputs(seed: int = 0) -> dict:
    seeds = jax.random.split(jax.random.key(seed), 11)
    return {
        "hidden": gaussian(seeds[0], (STEPS, RTOT, D), 1.0, 6.0, ((1, 128), (2, 8))),
        "queries": draw_queries(jax.random.fold_in(seeds[10], 71), 0),
        "cache_keys": draw_cache_keys(jax.random.fold_in(seeds[10], 71), 0),
        "cache_values": gaussian(seeds[3], (RTOT, CAP, KVD), 1.0, 6.0, ((0, 128), (2, 8))),
        "new_values": gaussian(seeds[4], (STEPS, RTOT, KVD), 1.0, 6.0, ((1, 128), (2, 8))),
        "lengths": draw_lengths(jax.random.fold_in(seeds[10], 71), 0),
        "base_weight": gaussian(seeds[6], (D, KVD), D ** -0.5, 0.046875, ((1, 8),)),
        "delta_values": gaussian(seeds[7], (D, KVD), 1.0, 4.0, ((0, 1024),)),
        "delta_scales": jnp.clip(jnp.exp(math.log(0.019897461) - 2.2979944 * jax.random.uniform(seeds[8], (NBR, KVD // BLK), jnp.float32) ** steps_of(seeds[8], (NBR, KVD // BLK), ((0, 128), (1, 8)), -0.2, 0.2)), 0.0019989014, 0.019897461).astype(jnp.bfloat16),
        "block_order": jax.random.permutation(seeds[9], NBR).astype(jnp.int32),
    }


def reference(hidden, queries, cache_keys, cache_values, new_values, lengths, base_weight, delta_values, delta_scales, block_order):
    positions = jnp.arange(NBR).astype(jnp.int32)
    inverse = lax.optimization_barrier(jnp.sum(jnp.where(block_order[None, :] == positions[:, None], positions[None, :], 0), axis=1)).astype(jnp.int32)
    blocks = delta_values.reshape(NBR, BLK, KVD // BLK, BLK).astype(jnp.float32) * delta_scales.astype(jnp.float32)[:, None, :, None]
    blocks = lax.optimization_barrier(blocks.astype(jnp.bfloat16))
    delta = jnp.take(blocks, inverse, axis=0).reshape(D, KVD)
    refreshed = (base_weight.astype(jnp.float32) + delta.astype(jnp.float32)).astype(jnp.bfloat16)
    keys_full = jnp.dot(hidden.reshape(STEPS * RTOT, D), refreshed, preferred_element_type=jnp.float32)
    new_keys = keys_full.reshape(STEPS, RTOT, KVD).astype(jnp.bfloat16)
    group = QH // KVH
    factor = 1.0 / math.sqrt(HD)
    cache_mask = jnp.arange(CAP)[None, :] < lengths[:, None]
    step_mask = jnp.arange(STEPS)[None, :] <= jnp.arange(STEPS)[:, None]

    def one_head(head):
        query = lax.dynamic_slice_in_dim(queries, head * group * HD, group * HD, 2)
        query = query.reshape(STEPS, RTOT, group, HD).astype(jnp.float32)
        ckeys = lax.dynamic_slice_in_dim(cache_keys, head * HD, HD, 2).astype(jnp.float32)
        cvals = lax.dynamic_slice_in_dim(cache_values, head * HD, HD, 2).astype(jnp.float32)
        nkeys = lax.dynamic_slice_in_dim(new_keys, head * HD, HD, 2).astype(jnp.float32)
        nvals = lax.dynamic_slice_in_dim(new_values, head * HD, HD, 2).astype(jnp.float32)
        cached = jnp.einsum('srgd,rcd->srgc', query, ckeys) * factor
        fresh = jnp.einsum('srgd,urd->srgu', query, nkeys) * factor
        cached = jnp.where(cache_mask[None, :, None, :], cached, -1e+30)
        fresh = jnp.where(step_mask[:, None, None, :], fresh, -1e+30)
        joined = jnp.concatenate([cached, fresh], axis=3)
        top = lax.optimization_barrier(jnp.max(joined, axis=3, keepdims=True))
        expo = jnp.exp(joined - top)
        weights = (expo / lax.optimization_barrier(jnp.sum(expo, axis=3, keepdims=True))).astype(jnp.bfloat16).astype(jnp.float32)
        result = jnp.einsum('srgc,rcd->srgd', weights[..., :CAP], cvals)
        result = result + jnp.einsum('srgu,urd->srgd', weights[..., CAP:], nvals)
        return result.astype(jnp.bfloat16)
    stacked = lax.map(one_head, jnp.arange(KVH).astype(jnp.int32))
    attended = jnp.transpose(stacked, (1, 2, 0, 3, 4)).reshape(STEPS, RTOT, QH * HD)
    return (attended, new_keys)
```

```python
import functools
import math

import jax
import jax.numpy as jnp
from jax import lax
from jax.experimental import pallas as pl
from jax.experimental.pallas import tpu as pltpu
from jax.sharding import PartitionSpec as P

HD = 128
TILE = 16
MESH = pl.DeviceIdType.MESH
F32 = jnp.float32
BF16 = jnp.bfloat16
GRID = {128: (8, 8, 2)}
NEG = -1e30


def contract(a, b, dims):
    return lax.dot_general(a, b, (dims, ((), ())), preferred_element_type=F32)


def kernel(
    dims,
    inverse_ref,
    lengths_ref,
    parcel_ref,
    delta_ref,
    hidden_hbm,
    queries_hbm,
    ckeys_hbm,
    cvals_hbm,
    nvals_ref,
    attended_ref,
    keys_ref,
    hidden_v,
    queries_v,
    ckeys_v,
    cvals_v,
    pick_v,
    regroup_v,
    hid_v,
    parcels_v,
    deltas_v,
    wide_v,
    *rest,
):
    nz, ny, nh, nt, rows = dims
    blocks = nz * ny * nh
    local_blocks = blocks // nt
    chips = nt // 2
    total = 2 * rows
    span = local_blocks * TILE
    width = nt * span
    heads = attended_ref.shape[2] // HD
    packs = rows // 8
    lines = 2 * heads * 8
    cap = ckeys_v.shape[1]
    keys8 = 8 * cap
    factor = 1.0 / math.sqrt(HD)

    w_v = rest[:chips]
    (
        partial_v,
        part_in_v,
        fresh_v,
        nval_v,
        q_v,
        o_v,
        m_v,
        l_v,
        mask_v,
        result_v,
        load_sem,
        p0_send,
        p0_recv,
        delta_send,
        delta_recv,
        hid_send,
        hid_recv,
        s1_send,
        s1_recv,
        s2_send,
        s2_recv,
        p6_send,
        p6_recv,
    ) = rest[chips:]

    f = lax.axis_index("fsdp")
    t = lax.axis_index("tp")
    h = lax.rem(f, nh)
    y = lax.rem(f // nh, ny)
    z = f // (nh * ny)

    def at(zz, yy, hh, tt):
        return ((zz * ny + yy) * nh + hh, tt)

    def y_peer(step):
        return at(z, lax.rem(y + step + ny, ny), h, t)

    def z_peer(step):
        return at(lax.rem(z + step + nz, nz), y, h, t)

    def x_peer(dh, d):
        return at(z, y, lax.rem(h + dh, nh), lax.rem(t + d, nt))

    x_peers = [(dh, d) for dh in range(nh) for d in range(nt) if (dh, d) != (0, 0)]

    loads = [
        pltpu.make_async_copy(src, dst, load_sem.at[i])
        for i, (src, dst) in enumerate(
            ((hidden_hbm, hidden_v), (queries_hbm, queries_v), (ckeys_hbm, ckeys_v), (cvals_hbm, cvals_v))
        )
    ]
    for load in loads:
        load.start()

    barrier = pltpu.get_barrier_semaphore()
    count = 0
    for peer in (
        [x_peer(*p) for p in x_peers]
        + [y_peer(s) for s in range(1, ny)]
        + [z_peer(s) for s in range(1, nz)]
    ):
        pl.semaphore_signal(barrier, inc=1, device_id=peer, device_id_type=MESH)
        count += 1
    pl.semaphore_wait(barrier, count)

    def remote(src, dst, send, recv, peer):
        return pltpu.make_async_remote_copy(
            src_ref=src, dst_ref=dst, send_sem=send, recv_sem=recv, device_id=peer, device_id_type=MESH
        )

    sent = []

    def start(copy):
        copy.start()
        sent.append(copy)

    for i, (dh, d) in enumerate(x_peers):
        start(
            remote(
                parcel_ref.at[lax.rem(t + d, nt)],
                parcels_v.at[h * nt + t],
                p0_send.at[i],
                p0_recv.at[i],
                x_peer(dh, d),
            )
        )
    if nh > 1:
        start(remote(delta_ref, deltas_v.at[h], delta_send, delta_recv, x_peer(1, 0)))
    parcels_v[h * nt + t] = parcel_ref[t]
    deltas_v[h] = delta_ref[...]

    lane_k = lax.broadcasted_iota(jnp.int32, (width, span), 0)
    lane_l = lax.broadcasted_iota(jnp.int32, (width, span), 1)
    target = (lane_k // (nt * TILE)) * TILE + lax.rem(lane_k, TILE)
    pick_v[...] = jnp.where(target == lane_l, 1.0, 0.0).astype(BF16)
    loads[0].wait()
    group_of = lax.rem(lax.broadcasted_iota(jnp.int32, (rows, width), 1) // TILE, nt)

    def regroup(g, carry):
        halves = []
        for s in range(2):
            chosen = jnp.where(group_of == g, hidden_v[s].astype(F32), 0.0).astype(BF16)
            halves.append(contract(chosen, pick_v[...], ((1,), (0,))))
        regroup_v[g] = jnp.concatenate(halves, axis=0).astype(BF16)
        return carry

    lax.fori_loop(0, nt, regroup, 0)
    for d in range(1, nt):
        start(
            remote(
                regroup_v.at[lax.rem(t + d, nt)],
                hid_v.at[t],
                hid_send.at[d],
                hid_recv.at[d],
                x_peer(0, d),
            )
        )
    hid_v[t] = regroup_v[t]

    for i, (dh, d) in enumerate(x_peers):
        source = lax.rem(h + nh - dh, nh) * nt + lax.rem(t + nt - d, nt)
        remote(parcel_ref.at[0], parcels_v.at[source], p0_send.at[i], p0_recv.at[i], x_peer(dh, d)).wait_recv()
    if nh > 1:
        remote(delta_ref, deltas_v.at[1 - h], delta_send, delta_recv, x_peer(1, 0)).wait_recv()

    def axes(c):
        if c < (chips + 1) // 2:
            return (y, ny, y_peer), (z, nz, z_peer)
        return (z, nz, z_peer), (y, ny, y_peer)

    for c in range(chips):
        (a, na, _), (b, nb, _) = axes(c)
        own = (b * na + a) * nh
        for hh in range(nh):
            cols = []
            for k in range(2):
                col = 2 * c + k
                parcel = parcels_v[hh * nt + col].astype(F32)
                scaled = deltas_v[hh, :, col * HD : (col + 1) * HD].astype(F32) * parcel[TILE:]
                scaled = scaled.astype(BF16).astype(F32)
                cols.append(parcel[:TILE] + scaled)
            w_v[c][own + hh] = jnp.concatenate(cols, axis=1).astype(BF16)

    order = []
    for i in range((chips + 1) // 2):
        pair = [i, chips - 1 - i]
        order.append(pair if pair[0] != pair[1] else pair[:1])

    def stage1_piece(c, source_a):
        (a, na, _), (b, nb, _) = axes(c)
        return w_v[c].at[pl.ds((b * na + source_a) * nh, nh)]

    def stage1_send(c):
        (a, na, peer), _ = axes(c)
        for s in range(1, na):
            start(remote(stage1_piece(c, a), stage1_piece(c, a), s1_send.at[c, s], s1_recv.at[c, s], peer(s)))

    def stage1_wait(c):
        (a, na, peer), _ = axes(c)
        for s in range(1, na):
            piece = stage1_piece(c, lax.rem(a + na - s, na))
            remote(piece, piece, s1_send.at[c, s], s1_recv.at[c, s], peer(s)).wait_recv()

    def unit(c, which, half):
        (a, na, _), (b, nb, _) = axes(c)
        size = na * nh // 2
        start_row = lax.rem(b + which + 2 * nb, nb) * (na * nh) + half * size
        return w_v[c].at[pl.ds(start_row, size)]

    def hops(c, way):
        nb = axes(c)[1][1]
        return nb // 2 if way == 0 else nb - 1 - nb // 2

    def sign(group, way):
        return 1 if (group + way) % 2 == 0 else -1

    def stage2_send(group, step, half):
        for c in order[group]:
            peer = axes(c)[1][2]
            for way in range(2):
                if step < hops(c, way):
                    sg = sign(group, way)
                    piece = unit(c, -sg * step, half)
                    start(
                        remote(
                            piece, piece, s2_send.at[c, way, step, half], s2_recv.at[c, way, step, half], peer(sg)
                        )
                    )

    def stage2_wait(group, step, half):
        for c in order[group]:
            peer = axes(c)[1][2]
            for way in range(2):
                if step < hops(c, way):
                    sg = sign(group, way)
                    piece = unit(c, -sg * (step + 1), half)
                    remote(
                        piece, piece, s2_send.at[c, way, step, half], s2_recv.at[c, way, step, half], peer(sg)
                    ).wait_recv()

    for pair in order:
        for c in pair:
            stage1_send(c)

    for load in loads[1:]:
        load.wait()
    wide_v[...] = queries_v[...].astype(F32)
    line = lax.broadcasted_iota(jnp.int32, (lines, keys8), 0)
    place = lax.broadcasted_iota(jnp.int32, (lines, keys8), 1)
    mask_v[...] = jnp.where(lax.rem(line, 8) == place // cap, 0.0, NEG)
    nval_v[...] = jnp.concatenate([nvals_ref[0].astype(F32), nvals_ref[1].astype(F32)], axis=0)

    def cached(i, carry):
        row = pl.multiple_of(i * 8, 8)
        parts = [
            wide_v[s, pl.ds(row, 8), g * HD : (g + 1) * HD] for s in range(2) for g in range(heads)
        ]
        q = jnp.concatenate(parts, axis=0).astype(BF16)
        q_v[i] = q
        k = ckeys_v[pl.ds(row, 8)].reshape(keys8, HD)
        v = cvals_v[pl.ds(row, 8)].reshape(keys8, HD)
        slot = lax.broadcasted_iota(jnp.int32, (1, keys8), 1)
        limit = jnp.zeros((1, keys8), jnp.int32)
        for r in range(8):
            limit = jnp.where(slot // cap == r, lengths_ref[row + r], limit)
        open_slot = lax.rem(slot, cap) < limit
        scores = contract(q, k, ((1,), (1,))) * factor
        scores = jnp.where(open_slot, scores + mask_v[...], NEG)
        top = jnp.max(scores, axis=1, keepdims=True)
        expo = jnp.exp(scores - top)
        o_v[i] = contract(expo.astype(BF16), v, ((1,), (0,)))
        m_v[i] = jnp.broadcast_to(top, (lines, HD))
        l_v[i] = jnp.broadcast_to(jnp.sum(expo, axis=1, keepdims=True), (lines, HD))
        return carry

    done = [0]

    def some_cached(upto):
        upto = min(upto, packs)
        if upto > done[0]:
            lax.fori_loop(done[0], upto, cached, 0)
            done[0] = upto

    def product(c):
        total_ = jnp.zeros((total, 2 * HD), F32)
        (_, na, _), (_, nb, _) = axes(c)
        kind = 0 if c < (chips + 1) // 2 else 1

        def step(k, acc):
            tiles = [w_v[c][inverse_ref[kind, k * local_blocks + j]] for j in range(local_blocks)]
            w = jnp.concatenate(tiles, axis=0)
            return acc + contract(hid_v[k], w, ((1,), (0,)))

        acc = lax.fori_loop(0, nt, step, total_)
        for k in range(2):
            owner = 2 * c + k
            partial_v[owner] = acc[:, k * HD : (k + 1) * HD]

            @pl.when(t != owner)
            def _():
                remote(
                    partial_v.at[owner],
                    part_in_v.at[t],
                    p6_send.at[owner],
                    p6_recv.at[lax.rem(owner - t + nt, nt)],
                    (f, owner),
                ).start()

    groups = len(order)
    steps = max(hops(c, 0) for c in range(chips))
    pending = []
    waited_hidden = False
    for group in range(groups):
        for c in order[group]:
            stage1_wait(c)
        for half in range(2):
            stage2_send(group, 0, half)
        if group > 0:
            for half in range(2):
                stage2_wait(group - 1, steps - 1, half)
            pending += order[group - 1]
        for step in range(1, steps):
            for half in range(2):
                if group == 0:
                    some_cached(-(-packs * (2 * step + half - 1) // max(1, 2 * (steps - 1))))
                stage2_wait(group, step - 1, half)
                stage2_send(group, step, half)
                if pending:
                    if not waited_hidden:
                        waited_hidden = True
                        for d in range(1, nt):
                            remote(
                                regroup_v.at[0],
                                hid_v.at[lax.rem(t + nt - d, nt)],
                                hid_send.at[d],
                                hid_recv.at[d],
                                x_peer(0, d),
                            ).wait_recv()
                    product(pending.pop(0))
    some_cached(packs)
    for half in range(2):
        stage2_wait(groups - 1, steps - 1, half)
    pending += order[groups - 1]
    if not waited_hidden:
        for d in range(1, nt):
            remote(
                regroup_v.at[0], hid_v.at[lax.rem(t + nt - d, nt)], hid_send.at[d], hid_recv.at[d], x_peer(0, d)
            ).wait_recv()
    for c in pending:
        product(c)

    for d in range(1, nt):
        remote(
            partial_v.at[0], part_in_v.at[lax.rem(t + nt - d, nt)], p6_send.at[0], p6_recv.at[d], x_peer(0, d)
        ).wait_recv()
    keys = partial_v[t]
    for d in range(1, nt):
        keys = keys + part_in_v[lax.rem(t + nt - d, nt)]
    keys16 = keys.astype(BF16)
    keys32 = keys16.astype(F32)
    fresh_v[...] = keys32
    keys_ref[0] = keys32[:rows].astype(BF16)
    keys_ref[1] = keys32[rows:].astype(BF16)

    line2 = lax.broadcasted_iota(jnp.int32, (lines, 16), 0)
    place2 = lax.broadcasted_iota(jnp.int32, (lines, 16), 1)
    allowed = (lax.rem(line2, 8) == lax.rem(place2, 8)) & (place2 // 8 <= line2 // (heads * 8))

    def finish(i, carry):
        row = pl.multiple_of(i * 8, 8)
        late = pl.multiple_of(rows + i * 8, 8)
        nk = jnp.concatenate([fresh_v[pl.ds(row, 8)], fresh_v[pl.ds(late, 8)]], axis=0).astype(BF16)
        nv = jnp.concatenate([nval_v[pl.ds(row, 8)], nval_v[pl.ds(late, 8)]], axis=0).astype(BF16)
        scores = jnp.where(allowed, contract(q_v[i], nk, ((1,), (1,))) * factor, NEG)
        old = m_v[i]
        top = jnp.maximum(old, jnp.max(scores, axis=1, keepdims=True))
        keep = jnp.exp(old - top)
        expo = jnp.exp(scores - top[:, :16])
        weight = l_v[i] * keep + jnp.sum(expo, axis=1, keepdims=True)
        out = (o_v[i] * keep + contract(expo.astype(BF16), nv, ((1,), (0,)))) / weight
        for s in range(2):
            for g in range(heads):
                at_line = (s * heads + g) * 8
                result_v[s, pl.ds(row, 8), g * HD : (g + 1) * HD] = out[at_line : at_line + 8]
        return carry

    lax.fori_loop(0, packs, finish, 0)
    attended_ref[...] = result_v[...].astype(BF16)

    for copy in sent:
        copy.wait_send()
    for owner in range(nt):

        @pl.when(t != owner)
        def _():
            remote(
                partial_v.at[owner], part_in_v.at[t], p6_send.at[owner], p6_recv.at[0], (f, owner)
            ).wait_send()


def per_device(
    grid,
    nt,
    hidden,
    queries,
    cache_keys,
    cache_values,
    new_values,
    lengths,
    base_weight,
    delta_values,
    delta_scales,
    block_order,
):
    nz, ny, nh = grid
    blocks = nz * ny * nh
    rows = hidden.shape[1]
    blk = base_weight.shape[0] // blocks
    assert blk == nt * TILE and base_weight.shape[1] == HD
    f = lax.axis_index("fsdp")
    block = lax.dynamic_slice_in_dim(base_weight, block_order[f] * blk, blk, 0)
    scale = jnp.broadcast_to(delta_scales.reshape(1, 1, 1), (nt, TILE, HD))
    parcel = jnp.concatenate([block.reshape(nt, TILE, HD), scale], axis=1)
    numbers = jnp.arange(blocks, dtype=jnp.int32)
    zz, yy, hh = numbers // (ny * nh), (numbers // nh) % ny, numbers % nh
    slots = jnp.stack([numbers, (yy * nz + zz) * nh + hh])
    inverse = jnp.sum(
        jnp.where(block_order[None, None, :] == numbers[None, :, None], slots[:, None, :], 0), axis=2
    ).astype(jnp.int32)

    chips = nt // 2
    total = 2 * rows
    span = blocks // nt * TILE
    width = nt * span
    heads = queries.shape[2] // HD
    packs = rows // 8
    lines = 2 * heads * 8
    cap = cache_keys.shape[1]
    ring = max(ny, nz)
    xs = nh * nt - 1
    dma = pltpu.SemaphoreType.DMA
    scratch = [
        pltpu.VMEM(hidden.shape, BF16),
        pltpu.VMEM(queries.shape, BF16),
        pltpu.VMEM(cache_keys.shape, BF16),
        pltpu.VMEM(cache_values.shape, BF16),
        pltpu.VMEM((width, span), BF16),
        pltpu.VMEM((nt, total, span), BF16),
        pltpu.VMEM((nt, total, span), BF16),
        pltpu.VMEM((nh * nt, 2 * TILE, HD), BF16),
        pltpu.VMEM((nh, TILE, nt * HD), BF16),
        pltpu.VMEM(queries.shape, F32),
        *[pltpu.VMEM((blocks, TILE, 2 * HD), BF16) for _ in range(chips)],
        pltpu.VMEM((nt, total, HD), F32),
        pltpu.VMEM((nt, total, HD), F32),
        pltpu.VMEM((total, HD), F32),
        pltpu.VMEM((total, HD), F32),
        pltpu.VMEM((packs, lines, HD), BF16),
        pltpu.VMEM((packs, lines, HD), F32),
        pltpu.VMEM((packs, lines, HD), F32),
        pltpu.VMEM((packs, lines, HD), F32),
        pltpu.VMEM((lines, 8 * cap), F32),
        pltpu.VMEM(queries.shape, F32),
        dma((4,)),
        dma((xs,)),
        dma((xs,)),
        dma,
        dma,
        dma((nt,)),
        dma((nt,)),
        dma((chips, ring)),
        dma((chips, ring)),
        dma((chips, 2, ring // 2, 2)),
        dma((chips, 2, ring // 2, 2)),
        dma((nt,)),
        dma((nt,)),
    ]
    vmem = pl.BlockSpec(memory_space=pltpu.VMEM)
    smem = pl.BlockSpec(memory_space=pltpu.SMEM)
    hbm = pl.BlockSpec(memory_space=pl.ANY)
    return tuple(
        pl.pallas_call(
            functools.partial(kernel, (nz, ny, nh, nt, rows)),
            out_shape=(
                jax.ShapeDtypeStruct(queries.shape, BF16),
                jax.ShapeDtypeStruct((2, rows, HD), BF16),
            ),
            in_specs=[smem, smem, vmem, vmem, hbm, hbm, hbm, hbm, vmem],
            out_specs=(vmem, vmem),
            scratch_shapes=scratch,
            compiler_params=pltpu.CompilerParams(
                collective_id=0, has_side_effects=True, vmem_limit_bytes=50 * 2**20
            ),
            name="refresh_project_attend",
        )(inverse, lengths, parcel, delta_values, hidden, queries, cache_keys, cache_values, new_values)
    )


def solution(mesh, grid=None):
    grid = grid or GRID[mesh.shape["fsdp"]]
    in_specs = (
        P(None, "fsdp", "tp"),
        P(None, "fsdp", "tp"),
        P("fsdp", None, "tp"),
        P("fsdp", None, "tp"),
        P(None, "fsdp", "tp"),
        P("fsdp"),
        P(None, "tp"),
        P(("fsdp", "tp"), None),
        P("fsdp", "tp"),
        P(),
    )
    out_specs = (P(None, "fsdp", "tp"), P(None, "fsdp", "tp"))
    return jax.shard_map(
        functools.partial(per_device, grid, mesh.shape["tp"]),
        mesh=mesh,
        in_specs=in_specs,
        out_specs=out_specs,
        check_vma=False,
    )
```

```python
import functools
import math

import jax
import jax.numpy as jnp
from jax import lax
from jax.experimental import pallas as pl
from jax.experimental.pallas import tpu as pltpu
from jax.sharding import PartitionSpec as P

HD = 128
TILE = 16
MESH = pl.DeviceIdType.MESH
F32 = jnp.float32
BF16 = jnp.bfloat16
GRID = {128: (8, 8, 2)}
NEG = -1e30
CUTS = 2


def contract(a, b, dims):
    return lax.dot_general(a, b, (dims, ((), ())), preferred_element_type=F32)


def kernel(
    dims,
    order_hbm,
    lengths_hbm,
    scale_hbm,
    base_hbm,
    delta_hbm,
    hidden_hbm,
    queries_hbm,
    ckeys_hbm,
    cvals_hbm,
    nvals_hbm,
    attended_ref,
    keys_ref,
    order_ref,
    lengths_ref,
    target_v,
    scale_v,
    base_v,
    delta_ref,
    nvals_ref,
    parcel_ref,
    hidden_v,
    queries_v,
    ckeys_v,
    cvals_v,
    hidden_all_v,
    pick_v,
    regroup_v,
    hid_v,
    parcels_v,
    deltas_v,
    wide_v,
    *rest,
):
    nz, ny, nh, nt, rows = dims
    blocks = nz * ny * nh
    local_blocks = blocks // nt
    chips = nt // 2
    total = 2 * rows
    sub = TILE // nh
    span = local_blocks * sub
    width = nt * nh * span
    heads = attended_ref.shape[2] // HD
    packs = rows // 8
    lines = 2 * heads * 8
    cap = ckeys_v.shape[1]
    keys8 = 8 * cap
    factor = 1.0 / math.sqrt(HD)

    bands = 2
    band_chips = chips // bands
    w_v = rest[:bands]
    (
        ordered_v,
        mine_v,
        give_v,
        take_v,
        out_v,
        part_in_v,
        fresh_v,
        nval_v,
        q_v,
        o_v,
        m_v,
        l_v,
        mask_v,
        result_v,
        load_sem,
        p0_send,
        p0_recv,
        delta_send,
        delta_recv,
        hid_send,
        hid_recv,
        s1_send,
        s1_recv,
        s2_send,
        s2_recv,
        pair_send,
        pair_recv,
        p6_send,
        p6_recv,
    ) = rest[bands:]

    f = lax.axis_index("fsdp")
    t = lax.axis_index("tp")
    h = lax.rem(f, nh)
    y = lax.rem(f // nh, ny)
    z = f // (nh * ny)

    def at(zz, yy, hh, tt):
        return ((zz * ny + yy) * nh + hh, tt)

    def y_peer(step):
        return at(z, lax.rem(y + step + ny, ny), h, t)

    def z_peer(step):
        return at(lax.rem(z + step + nz, nz), y, h, t)

    def x_peer(dh, d):
        return at(z, y, lax.rem(h + dh, nh), lax.rem(t + d, nt))

    x_peers = [(dh, d) for dh in range(nh) for d in range(nt) if (dh, d) != (0, 0)]

    loads = [
        pltpu.make_async_copy(src, dst, load_sem.at[i])
        for i, (src, dst) in enumerate(
            (
                (order_hbm, order_ref),
                (scale_hbm, scale_v),
                (base_hbm, base_v),
                (delta_hbm, delta_ref),
                (hidden_hbm, hidden_v),
                (lengths_hbm, lengths_ref),
                (queries_hbm, queries_v),
                (ckeys_hbm, ckeys_v),
                (cvals_hbm, cvals_v),
                (nvals_hbm, nvals_ref),
            )
        )
    ]
    for load in loads:
        load.start()

    barrier = pltpu.get_barrier_semaphore()
    count = 0
    for peer in (
        [x_peer(*p) for p in x_peers]
        + [y_peer(s) for s in range(1, ny)]
        + [z_peer(s) for s in range(1, nz)]
    ):
        pl.semaphore_signal(barrier, inc=1, device_id=peer, device_id_type=MESH)
        count += 1
    for load in loads[:4]:
        load.wait()
    parcel_ref[:, :TILE] = base_v[order_ref[f]].reshape(nt, TILE, HD)
    parcel_ref[:, TILE:] = jnp.broadcast_to(scale_v[...].reshape(1, 1, 1), (nt, TILE, HD))
    pl.semaphore_wait(barrier, count)

    def remote(src, dst, send, recv, peer):
        return pltpu.make_async_remote_copy(
            src_ref=src, dst_ref=dst, send_sem=send, recv_sem=recv, device_id=peer, device_id_type=MESH
        )

    sent = []

    def start(copy):
        copy.start()
        sent.append(copy)

    for i, (dh, d) in enumerate(x_peers):
        start(
            remote(
                parcel_ref.at[lax.rem(t + d, nt)],
                parcels_v.at[h * nt + t],
                p0_send.at[i],
                p0_recv.at[i],
                x_peer(dh, d),
            )
        )
    if nh > 1:
        start(remote(delta_ref, deltas_v.at[h], delta_send, delta_recv, x_peer(1, 0)))
    parcels_v[h * nt + t] = parcel_ref[t]
    deltas_v[h] = delta_ref[...]

    lane_k = lax.broadcasted_iota(jnp.int32, (width, nh * span), 0)
    lane_l = lax.broadcasted_iota(jnp.int32, (width, nh * span), 1)
    target = lax.rem(lane_k, TILE) // sub * span + lane_k // (nt * TILE) * sub + lax.rem(lane_k, sub)
    pick_v[...] = jnp.where(target == lane_l, 1.0, 0.0).astype(BF16)
    loads[4].wait()
    hidden_all_v[...] = jnp.concatenate([hidden_v[0].astype(F32), hidden_v[1].astype(F32)], axis=0).astype(BF16)
    group_of = lax.rem(lax.broadcasted_iota(jnp.int32, (1, width), 1) // TILE, nt)

    def regroup(g, carry):
        chosen = hidden_all_v[...] * jnp.where(group_of == g, 1.0, 0.0).astype(BF16)
        out = contract(chosen, pick_v[...], ((1,), (0,))).astype(BF16)
        for hh in range(nh):
            regroup_v[hh * nt + g] = out[:, hh * span : (hh + 1) * span]
        return carry

    lax.fori_loop(0, nt, regroup, 0)
    for i, (dh, d) in enumerate(x_peers):
        start(
            remote(
                regroup_v.at[lax.rem(h + dh, nh) * nt + lax.rem(t + d, nt)],
                hid_v.at[h * nt + t],
                hid_send.at[i],
                hid_recv.at[i],
                x_peer(dh, d),
            )
        )
    hid_v[h * nt + t] = regroup_v[h * nt + t]

    def hidden_wait():
        for i, (dh, d) in enumerate(x_peers):
            source = lax.rem(h + nh - dh, nh) * nt + lax.rem(t + nt - d, nt)
            remote(regroup_v.at[0], hid_v.at[source], hid_send.at[i], hid_recv.at[i], x_peer(dh, d)).wait_recv()

    for i, (dh, d) in enumerate(x_peers):
        source = lax.rem(h + nh - dh, nh) * nt + lax.rem(t + nt - d, nt)
        remote(parcel_ref.at[0], parcels_v.at[source], p0_send.at[i], p0_recv.at[i], x_peer(dh, d)).wait_recv()
    if nh > 1:
        remote(delta_ref, deltas_v.at[1 - h], delta_send, delta_recv, x_peer(1, 0)).wait_recv()

    def axes(c):
        if c == 0:
            return (y, ny, y_peer), (z, nz, z_peer)
        return (z, nz, z_peer), (y, ny, y_peer)

    def half_of(rows16):
        out = rows16[:sub]
        for hh in range(1, nh):
            out = jnp.where(h == hh, rows16[hh * sub : (hh + 1) * sub], out)
        return out

    for c in range(bands):
        (a, na, _), (b, nb, _) = axes(c)
        cols = []
        for col in range(c * nt // bands, (c + 1) * nt // bands):
            parts = []
            for hh in range(nh):
                parcel = parcels_v[hh * nt + col].astype(F32)
                update = deltas_v[hh, :, col * HD : (col + 1) * HD].astype(F32)
                scaled = (half_of(update) * parcel[TILE : TILE + sub]).astype(BF16).astype(F32)
                parts.append(half_of(parcel[:TILE]) + scaled)
            cols.append(jnp.concatenate(parts, axis=0))
        w_v[c][b * na + a] = jnp.concatenate(cols, axis=1).astype(BF16)

    def stage1_piece(c, source_a):
        (a, na, _), (b, nb, _) = axes(c)
        return w_v[c].at[pl.ds(b * na + source_a, 1)]

    def stage1_send(c):
        (a, na, peer), _ = axes(c)
        for s in range(1, na):
            start(remote(stage1_piece(c, a), stage1_piece(c, a), s1_send.at[c, s], s1_recv.at[c, s], peer(s)))

    def stage1_wait(c):
        (a, na, peer), _ = axes(c)
        for s in range(1, na):
            piece = stage1_piece(c, lax.rem(a + na - s, na))
            remote(piece, piece, s1_send.at[c, s], s1_recv.at[c, s], peer(s)).wait_recv()

    def unit(c, which, half):
        (a, na, _), (b, nb, _) = axes(c)
        size = na // CUTS
        start_row = lax.rem(b + which + 2 * nb, nb) * na + half * size
        return w_v[c].at[pl.ds(start_row, size)]

    def hops(c, way, half):
        nb = axes(c)[1][1]
        return nb // 2 if (half < CUTS // 2) == (way == 0) else nb - 1 - nb // 2

    def stage2_each(step, half, ahead, act):
        for c in range(bands):
            peer = axes(c)[1][2]
            for way, sign in enumerate((1, -1)):
                if step < hops(c, way, half):
                    piece = unit(c, -sign * (step + ahead), half)
                    act(
                        remote(
                            piece, piece, s2_send.at[c, way, step, half], s2_recv.at[c, way, step, half], peer(sign)
                        )
                    )

    def stage2_send(step, half):
        stage2_each(step, half, 0, start)

    def stage2_wait(step, half):
        stage2_each(step, half, 1, lambda copy: copy.wait_recv())

    for c in range(bands):
        stage1_send(c)

    for load in loads[5:]:
        load.wait()
    wide_v[...] = queries_v[...].astype(F32)
    line = lax.broadcasted_iota(jnp.int32, (lines, keys8), 0)
    place = lax.broadcasted_iota(jnp.int32, (lines, keys8), 1)
    mask_v[...] = jnp.where(lax.rem(line, 8) == place // cap, 0.0, NEG)
    nval_v[...] = jnp.concatenate([nvals_ref[0].astype(F32), nvals_ref[1].astype(F32)], axis=0)

    place_l = lax.broadcasted_iota(jnp.int32, (1, blocks * sub), 1)

    def aim(p, row):
        return jnp.where(place_l // sub == p, order_ref[p] * sub, row)

    aimed = lax.fori_loop(0, blocks, aim, jnp.zeros((1, blocks * sub), jnp.int32))
    target_v[...] = aimed + lax.rem(place_l, sub)

    def cached(i, carry):
        row = pl.multiple_of(i * 8, 8)
        parts = [
            wide_v[s, pl.ds(row, 8), g * HD : (g + 1) * HD] for s in range(2) for g in range(heads)
        ]
        q = jnp.concatenate(parts, axis=0).astype(BF16)
        q_v[i] = q
        k = ckeys_v[pl.ds(row, 8)].reshape(keys8, HD)
        v = cvals_v[pl.ds(row, 8)].reshape(keys8, HD)
        slot = lax.broadcasted_iota(jnp.int32, (1, keys8), 1)
        limit = jnp.zeros((1, keys8), jnp.int32)
        for r in range(8):
            limit = jnp.where(slot // cap == r, lengths_ref[row + r], limit)
        open_slot = lax.rem(slot, cap) < limit
        scores = contract(q, k, ((1,), (1,))) * factor
        scores = jnp.where(open_slot, scores + mask_v[...], NEG)
        top = jnp.max(scores, axis=1, keepdims=True)
        expo = jnp.exp(scores - top)
        o_v[i] = contract(expo.astype(BF16), v, ((1,), (0,)))
        m_v[i] = jnp.broadcast_to(top, (lines, HD))
        l_v[i] = jnp.broadcast_to(jnp.sum(expo, axis=1, keepdims=True), (lines, HD))
        return carry

    done = [0]

    def some_cached(upto):
        upto = min(upto, packs)
        if upto > done[0]:
            lax.fori_loop(done[0], upto, cached, 0)
            done[0] = upto

    def reorder():
        lanes = [
            jnp.concatenate([hid_v[hh * nt + k] for k in range(nt)], axis=1) for hh in range(nh)
        ]
        natural = jnp.concatenate(lanes, axis=0)
        depth = blocks * sub
        lanes_at = min(256, depth)
        line_ = lax.broadcasted_iota(jnp.int32, (depth, lanes_at), 0)
        for n in range(0, depth, lanes_at):
            pick = jnp.where(line_ == target_v[:, n : n + lanes_at], 1.0, 0.0).astype(BF16)
            ordered_v[:, n : n + lanes_at] = contract(natural, pick, ((1,), (0,))).astype(BF16)

    core = lax.rem(t, 2)
    chip = t // 2
    sibling = t + 1 - 2 * core

    def pair_copy(c):
        own = pl.ds(c * band_chips, band_chips)
        return remote(give_v.at[own], take_v.at[own], pair_send.at[c], pair_recv.at[c], (f, sibling))

    def product(c):
        depth = 2 * ny * TILE
        acc = None
        for k in range(nz // 2):
            if c == 0:
                w = w_v[c][2 * k * ny : (2 * k + 2) * ny].reshape(depth, band_chips * 2 * HD)
            else:
                w = jnp.concatenate(
                    [w_v[c][yy * nz + zz] for zz in (2 * k, 2 * k + 1) for yy in range(ny)], axis=0
                )
            term = contract(ordered_v[:, k * depth : (k + 1) * depth], w, ((1,), (0,)))
            acc = term if acc is None else acc + term
        for j in range(band_chips):
            one = acc[:, 2 * j * HD : (2 * j + 1) * HD]
            two = acc[:, (2 * j + 1) * HD : (2 * j + 2) * HD]
            mine_v[c * band_chips + j] = jnp.where(core == 0, one, two)
            give_v[c * band_chips + j] = jnp.where(core == 0, two, one)
        start(pair_copy(c))

    def to_owner(c, dh):
        hh = lax.rem(h + dh, nh)
        return remote(
            out_v.at[c, pl.ds(pl.multiple_of(hh * total, 16), total)],
            part_in_v.at[h * chips + chip],
            p6_send.at[c, dh],
            p6_recv.at[dh * chips + lax.rem(c - chip + chips, chips)],
            at(z, y, hh, 2 * c + core),
        )

    def each_owner(c, act):
        for dh in range(nh):
            if dh:
                act(to_owner(c, dh))
            else:

                @pl.when(chip != c)
                def _():
                    act(to_owner(c, 0))

    def combine(band):
        pair_copy(band).wait_recv()
        for c in range(band * band_chips, (band + 1) * band_chips):
            both = mine_v[c] + take_v[c]
            mine_v[c] = both
            out_v[c] = both.astype(BF16)
            each_owner(c, lambda copy: copy.start())

    steps = max(ny, nz) // 2
    for c in range(bands):
        stage1_wait(c)
    for half in range(CUTS):
        stage2_send(0, half)
    for step in range(1, steps):
        for half in range(CUTS):
            some_cached(-(-packs * (CUTS * (step - 1) + half + 1) // (CUTS * (steps - 1))))
            stage2_wait(step - 1, half)
            stage2_send(step, half)
    some_cached(packs)
    hidden_wait()
    reorder()
    for half in range(CUTS):
        stage2_wait(steps - 1, half)
    for c in range(bands):
        product(c)
    for c in range(bands):
        combine(c)

    keys = mine_v[chip, pl.ds(pl.multiple_of(h * total, 16), total)]
    for dh in range(nh):
        for d in range(chips):
            if (dh, d) != (0, 0):
                source = lax.rem(h + nh - dh, nh) * chips + lax.rem(chip + chips - d, chips)
                into = part_in_v.at[source]
                remote(into, into, p6_send.at[0, 0], p6_recv.at[dh * chips + d], (f, sibling)).wait_recv()
                keys = keys + part_in_v[source].astype(F32)
    keys16 = keys.astype(BF16)
    keys32 = keys16.astype(F32)
    fresh_v[...] = keys32
    keys_ref[0] = keys32[:rows].astype(BF16)
    keys_ref[1] = keys32[rows:].astype(BF16)

    line2 = lax.broadcasted_iota(jnp.int32, (lines, 16), 0)
    place2 = lax.broadcasted_iota(jnp.int32, (lines, 16), 1)
    allowed = (lax.rem(line2, 8) == lax.rem(place2, 8)) & (place2 // 8 <= line2 // (heads * 8))

    def finish(i, carry):
        row = pl.multiple_of(i * 8, 8)
        late = pl.multiple_of(rows + i * 8, 8)
        nk = jnp.concatenate([fresh_v[pl.ds(row, 8)], fresh_v[pl.ds(late, 8)]], axis=0).astype(BF16)
        nv = jnp.concatenate([nval_v[pl.ds(row, 8)], nval_v[pl.ds(late, 8)]], axis=0).astype(BF16)
        scores = jnp.where(allowed, contract(q_v[i], nk, ((1,), (1,))) * factor, NEG)
        old = m_v[i]
        top = jnp.maximum(old, jnp.max(scores, axis=1, keepdims=True))
        keep = jnp.exp(old - top)
        expo = jnp.exp(scores - top[:, :16])
        weight = l_v[i] * keep + jnp.sum(expo, axis=1, keepdims=True)
        out = (o_v[i] * keep + contract(expo.astype(BF16), nv, ((1,), (0,)))) / weight
        for s in range(2):
            for g in range(heads):
                at_line = (s * heads + g) * 8
                result_v[s, pl.ds(row, 8), g * HD : (g + 1) * HD] = out[at_line : at_line + 8]
        return carry

    lax.fori_loop(0, packs, finish, 0)
    attended_ref[...] = result_v[...].astype(BF16)

    for copy in sent:
        copy.wait_send()
    for c in range(chips):
        each_owner(c, lambda copy: copy.wait_send())


def per_device(
    grid,
    nt,
    hidden,
    queries,
    cache_keys,
    cache_values,
    new_values,
    lengths,
    base_weight,
    delta_values,
    delta_scales,
    block_order,
):
    nz, ny, nh = grid
    blocks = nz * ny * nh
    rows = hidden.shape[1]
    blk = base_weight.shape[0] // blocks
    assert blk == nt * TILE and base_weight.shape[1] == HD
    chips = nt // 2
    total = 2 * rows
    assert nh == 2
    span = blocks // nt * TILE // nh
    width = nt * nh * span
    heads = queries.shape[2] // HD
    packs = rows // 8
    lines = 2 * heads * 8
    cap = cache_keys.shape[1]
    ring = max(ny, nz)
    xs = nh * nt - 1
    dma = pltpu.SemaphoreType.DMA
    smem = pltpu.SMEM
    scratch = [
        smem(block_order.shape, jnp.int32),
        smem(lengths.shape, jnp.int32),
        pltpu.VMEM((1, blocks * TILE // nh), jnp.int32),
        pltpu.VMEM((1, 1), BF16),
        pltpu.VMEM((blocks, blk, HD), BF16),
        pltpu.VMEM(delta_values.shape, BF16),
        pltpu.VMEM(new_values.shape, BF16),
        pltpu.VMEM((nt, 2 * TILE, HD), BF16),
        pltpu.VMEM(hidden.shape, BF16),
        pltpu.VMEM(queries.shape, BF16),
        pltpu.VMEM(cache_keys.shape, BF16),
        pltpu.VMEM(cache_values.shape, BF16),
        pltpu.VMEM((total, width), BF16),
        pltpu.VMEM((width, nh * span), BF16),
        pltpu.VMEM((nh * nt, total, span), BF16),
        pltpu.VMEM((nh * nt, total, span), BF16),
        pltpu.VMEM((nh * nt, 2 * TILE, HD), BF16),
        pltpu.VMEM((nh, TILE, nt * HD), BF16),
        pltpu.VMEM(queries.shape, F32),
        *[pltpu.VMEM((blocks // nh, TILE, nt * HD // 2), BF16) for _ in range(2)],
        pltpu.VMEM((nh * total, blocks * TILE // nh), BF16),
        pltpu.VMEM((chips, nh * total, HD), F32),
        pltpu.VMEM((chips, nh * total, HD), F32),
        pltpu.VMEM((chips, nh * total, HD), F32),
        pltpu.VMEM((chips, nh * total, HD), BF16),
        pltpu.VMEM((nh * chips, total, HD), BF16),
        pltpu.VMEM((total, HD), F32),
        pltpu.VMEM((total, HD), F32),
        pltpu.VMEM((packs, lines, HD), BF16),
        pltpu.VMEM((packs, lines, HD), F32),
        pltpu.VMEM((packs, lines, HD), F32),
        pltpu.VMEM((packs, lines, HD), F32),
        pltpu.VMEM((lines, 8 * cap), F32),
        pltpu.VMEM(queries.shape, F32),
        dma((10,)),
        dma((xs,)),
        dma((xs,)),
        dma,
        dma,
        dma((xs,)),
        dma((xs,)),
        dma((2, ring)),
        dma((2, ring)),
        dma((2, 2, ring // 2, CUTS)),
        dma((2, 2, ring // 2, CUTS)),
        dma((2,)),
        dma((2,)),
        dma((chips, nh)),
        dma((nh * chips,)),
    ]
    vmem = pl.BlockSpec(memory_space=pltpu.VMEM)
    hbm = pl.BlockSpec(memory_space=pltpu.HBM)
    return tuple(
        pl.pallas_call(
            functools.partial(kernel, (nz, ny, nh, nt, rows)),
            out_shape=(
                jax.ShapeDtypeStruct(queries.shape, BF16),
                jax.ShapeDtypeStruct((2, rows, HD), BF16),
            ),
            in_specs=[hbm] * 10,
            out_specs=(vmem, vmem),
            scratch_shapes=scratch,
            compiler_params=pltpu.CompilerParams(
                collective_id=0, has_side_effects=True, vmem_limit_bytes=63 * 2**20
            ),
            name="refresh_project_attend",
        )(
            block_order,
            lengths,
            delta_scales,
            base_weight.reshape(blocks, blk, HD),
            delta_values,
            hidden,
            queries,
            cache_keys,
            cache_values,
            new_values,
        )
    )


def solution(mesh, grid=None):
    grid = grid or GRID[mesh.shape["fsdp"]]
    in_specs = (
        P(None, "fsdp", "tp"),
        P(None, "fsdp", "tp"),
        P("fsdp", None, "tp"),
        P("fsdp", None, "tp"),
        P(None, "fsdp", "tp"),
        P("fsdp"),
        P(None, "tp"),
        P(("fsdp", "tp"), None),
        P("fsdp", "tp"),
        P(),
    )
    out_specs = (P(None, "fsdp", "tp"), P(None, "fsdp", "tp"))
    return jax.shard_map(
        functools.partial(per_device, grid, mesh.shape["tp"]),
        mesh=mesh,
        in_specs=in_specs,
        out_specs=out_specs,
        check_vma=False,
    )
```

```python
import functools
import math

import jax
import jax.numpy as jnp
from jax import lax
from jax.experimental import pallas as pl
from jax.experimental.pallas import tpu as pltpu
from jax.sharding import PartitionSpec as P

HD = 128
TILE = 16
MESH = pl.DeviceIdType.MESH
F32 = jnp.float32
BF16 = jnp.bfloat16
GRID = {128: (8, 8, 2)}
NEG = -1e30
CUTS = 4


def contract(a, b, dims):
    return lax.dot_general(a, b, (dims, ((), ())), preferred_element_type=F32)


def kernel(
    dims,
    order_hbm,
    lengths_hbm,
    scale_hbm,
    base_hbm,
    delta_hbm,
    hidden_hbm,
    queries_hbm,
    ckeys_hbm,
    cvals_hbm,
    nvals_hbm,
    attended_ref,
    keys_ref,
    order_ref,
    lengths_ref,
    target_v,
    scale_v,
    base_v,
    delta_ref,
    nvals_ref,
    parcel_ref,
    hidden_v,
    queries_v,
    ckeys_v,
    cvals_v,
    hidden_all_v,
    pick_v,
    regroup_v,
    hid_v,
    parcels_v,
    deltas_v,
    wide_v,
    *rest,
):
    nz, ny, nh, nt, rows = dims
    blocks = nz * ny * nh
    local_blocks = blocks // nt
    chips = nt // 2
    total = 2 * rows
    sub = TILE // nh
    span = local_blocks * sub
    width = nt * nh * span
    heads = attended_ref.shape[2] // HD
    packs = rows // 8
    lines = 2 * heads * 8
    cap = ckeys_v.shape[1]
    keys8 = 8 * cap
    factor = 1.0 / math.sqrt(HD)

    bands = 2
    band_chips = chips // bands
    w_v = rest[:bands]
    (
        ordered_v,
        mine_v,
        give_v,
        take_v,
        out_v,
        part_in_v,
        fresh_v,
        nval_v,
        q_v,
        o_v,
        m_v,
        l_v,
        mask_v,
        result_v,
        load_sem,
        p0_send,
        p0_recv,
        delta_send,
        delta_recv,
        hid_send,
        hid_recv,
        s1_send,
        s1_recv,
        s2_send,
        s2_recv,
        pair_send,
        pair_recv,
        p6_send,
        p6_recv,
    ) = rest[bands:]

    f = lax.axis_index("fsdp")
    t = lax.axis_index("tp")
    h = lax.rem(f, nh)
    y = lax.rem(f // nh, ny)
    z = f // (nh * ny)

    def at(zz, yy, hh, tt):
        return ((zz * ny + yy) * nh + hh, tt)

    def y_peer(step):
        return at(z, lax.rem(y + step + ny, ny), h, t)

    def z_peer(step):
        return at(lax.rem(z + step + nz, nz), y, h, t)

    def x_peer(dh, d):
        return at(z, y, lax.rem(h + dh, nh), lax.rem(t + d, nt))

    x_peers = [(dh, d) for dh in range(nh) for d in range(nt) if (dh, d) != (0, 0)]

    loads = [
        pltpu.make_async_copy(src, dst, load_sem.at[i])
        for i, (src, dst) in enumerate(
            (
                (order_hbm, order_ref),
                (scale_hbm, scale_v),
                (base_hbm, base_v),
                (delta_hbm, delta_ref),
                (hidden_hbm, hidden_v),
                (lengths_hbm, lengths_ref),
                (queries_hbm, queries_v),
                (ckeys_hbm, ckeys_v),
                (cvals_hbm, cvals_v),
                (nvals_hbm, nvals_ref),
            )
        )
    ]
    for load in loads[:4]:
        load.start()

    barrier = pltpu.get_barrier_semaphore()
    count = 0
    for peer in (
        [x_peer(*p) for p in x_peers]
        + [y_peer(s) for s in range(1, ny)]
        + [z_peer(s) for s in range(1, nz)]
    ):
        pl.semaphore_signal(barrier, inc=1, device_id=peer, device_id_type=MESH)
        count += 1
    for load in loads[:4]:
        load.wait()
    for load in loads[4:]:
        load.start()
    parcel_ref[:, :TILE] = base_v[order_ref[f]].reshape(nt, TILE, HD)
    parcel_ref[:, TILE:] = jnp.broadcast_to(scale_v[...].reshape(1, 1, 1), (nt, TILE, HD))
    pl.semaphore_wait(barrier, count)

    def remote(src, dst, send, recv, peer):
        return pltpu.make_async_remote_copy(
            src_ref=src, dst_ref=dst, send_sem=send, recv_sem=recv, device_id=peer, device_id_type=MESH
        )

    sent = []

    def start(copy):
        copy.start()
        sent.append(copy)

    for i, (dh, d) in enumerate(x_peers):
        start(
            remote(
                parcel_ref.at[lax.rem(t + d, nt)],
                parcels_v.at[h * nt + t],
                p0_send.at[i],
                p0_recv.at[i],
                x_peer(dh, d),
            )
        )
    if nh > 1:
        start(remote(delta_ref, deltas_v.at[h], delta_send, delta_recv, x_peer(1, 0)))
    parcels_v[h * nt + t] = parcel_ref[t]
    deltas_v[h] = delta_ref[...]

    def hidden_wait():
        for i, (dh, d) in enumerate(x_peers):
            source = lax.rem(h + nh - dh, nh) * nt + lax.rem(t + nt - d, nt)
            remote(regroup_v.at[0], hid_v.at[source], hid_send.at[i], hid_recv.at[i], x_peer(dh, d)).wait_recv()

    for i, (dh, d) in enumerate(x_peers):
        source = lax.rem(h + nh - dh, nh) * nt + lax.rem(t + nt - d, nt)
        remote(parcel_ref.at[0], parcels_v.at[source], p0_send.at[i], p0_recv.at[i], x_peer(dh, d)).wait_recv()
    if nh > 1:
        remote(delta_ref, deltas_v.at[1 - h], delta_send, delta_recv, x_peer(1, 0)).wait_recv()

    def axes(c):
        if c == 0:
            return (y, ny, y_peer), (z, nz, z_peer)
        return (z, nz, z_peer), (y, ny, y_peer)

    def half_of(rows16):
        out = rows16[:sub]
        for hh in range(1, nh):
            out = jnp.where(h == hh, rows16[hh * sub : (hh + 1) * sub], out)
        return out

    for c in range(bands):
        (a, na, _), (b, nb, _) = axes(c)
        cols = []
        for col in range(c * nt // bands, (c + 1) * nt // bands):
            parts = []
            for hh in range(nh):
                parcel = parcels_v[hh * nt + col].astype(F32)
                update = deltas_v[hh, :, col * HD : (col + 1) * HD].astype(F32)
                scaled = (half_of(update) * parcel[TILE : TILE + sub]).astype(BF16).astype(F32)
                parts.append(half_of(parcel[:TILE]) + scaled)
            cols.append(jnp.concatenate(parts, axis=0))
        w_v[c][b * na + a] = jnp.concatenate(cols, axis=1).astype(BF16)

    def stage1_piece(c, source_a):
        (a, na, _), (b, nb, _) = axes(c)
        return w_v[c].at[pl.ds(b * na + source_a, 1)]

    def stage1_send(c):
        (a, na, peer), _ = axes(c)
        for s in range(1, na):
            start(remote(stage1_piece(c, a), stage1_piece(c, a), s1_send.at[c, s], s1_recv.at[c, s], peer(s)))

    def stage1_wait(c):
        (a, na, peer), _ = axes(c)
        for s in range(1, na):
            piece = stage1_piece(c, lax.rem(a + na - s, na))
            remote(piece, piece, s1_send.at[c, s], s1_recv.at[c, s], peer(s)).wait_recv()

    def unit(c, which, half):
        (a, na, _), (b, nb, _) = axes(c)
        size = na // CUTS
        start_row = lax.rem(b + which + 2 * nb, nb) * na + half * size
        return w_v[c].at[pl.ds(start_row, size)]

    def hops(c, way, half):
        nb = axes(c)[1][1]
        return nb // 2 if (half < CUTS // 2) == (way == 0) else nb - 1 - nb // 2

    def stage2_each(step, half, ahead, act):
        for c in range(bands):
            peer = axes(c)[1][2]
            for way, sign in enumerate((1, -1)):
                if step < hops(c, way, half):
                    piece = unit(c, -sign * (step + ahead), half)
                    act(
                        remote(
                            piece, piece, s2_send.at[c, way, step, half], s2_recv.at[c, way, step, half], peer(sign)
                        )
                    )

    def stage2_send(step, half):
        stage2_each(step, half, 0, start)

    def stage2_wait(step, half):
        stage2_each(step, half, 1, lambda copy: copy.wait_recv())

    for c in range(bands):
        stage1_send(c)

    lane_k = lax.broadcasted_iota(jnp.int32, (width, nh * span), 0)
    lane_l = lax.broadcasted_iota(jnp.int32, (width, nh * span), 1)
    target = lax.rem(lane_k, TILE) // sub * span + lane_k // (nt * TILE) * sub + lax.rem(lane_k, sub)
    pick_v[...] = jnp.where(target == lane_l, 1.0, 0.0).astype(BF16)
    loads[4].wait()
    hidden_all_v[...] = jnp.concatenate([hidden_v[0].astype(F32), hidden_v[1].astype(F32)], axis=0).astype(BF16)
    group_of = lax.rem(lax.broadcasted_iota(jnp.int32, (1, width), 1) // TILE, nt)

    def regroup(g, carry):
        chosen = hidden_all_v[...] * jnp.where(group_of == g, 1.0, 0.0).astype(BF16)
        out = contract(chosen, pick_v[...], ((1,), (0,))).astype(BF16)
        for hh in range(nh):
            regroup_v[hh * nt + g] = out[:, hh * span : (hh + 1) * span]
        return carry

    lax.fori_loop(0, nt, regroup, 0)
    for i, (dh, d) in enumerate(x_peers):
        start(
            remote(
                regroup_v.at[lax.rem(h + dh, nh) * nt + lax.rem(t + d, nt)],
                hid_v.at[h * nt + t],
                hid_send.at[i],
                hid_recv.at[i],
                x_peer(dh, d),
            )
        )
    hid_v[h * nt + t] = regroup_v[h * nt + t]

    for load in loads[5:]:
        load.wait()
    wide_v[...] = queries_v[...].astype(F32)
    line = lax.broadcasted_iota(jnp.int32, (lines, keys8), 0)
    place = lax.broadcasted_iota(jnp.int32, (lines, keys8), 1)
    mask_v[...] = jnp.where(lax.rem(line, 8) == place // cap, 0.0, NEG)
    nval_v[...] = jnp.concatenate([nvals_ref[0].astype(F32), nvals_ref[1].astype(F32)], axis=0)

    place_l = lax.broadcasted_iota(jnp.int32, (1, blocks * sub), 1)

    def aim(p, row):
        return jnp.where(place_l // sub == p, order_ref[p] * sub, row)

    aimed = lax.fori_loop(0, blocks, aim, jnp.zeros((1, blocks * sub), jnp.int32))
    target_v[...] = aimed + lax.rem(place_l, sub)

    def cached(i, carry):
        row = pl.multiple_of(i * 8, 8)
        parts = [
            wide_v[s, pl.ds(row, 8), g * HD : (g + 1) * HD] for s in range(2) for g in range(heads)
        ]
        q = jnp.concatenate(parts, axis=0).astype(BF16)
        q_v[i] = q
        k = ckeys_v[pl.ds(row, 8)].reshape(keys8, HD)
        v = cvals_v[pl.ds(row, 8)].reshape(keys8, HD)
        slot = lax.broadcasted_iota(jnp.int32, (1, keys8), 1)
        limit = jnp.zeros((1, keys8), jnp.int32)
        for r in range(8):
            limit = jnp.where(slot // cap == r, lengths_ref[row + r], limit)
        open_slot = lax.rem(slot, cap) < limit
        scores = contract(q, k, ((1,), (1,))) * factor
        scores = jnp.where(open_slot, scores + mask_v[...], NEG)
        top = jnp.max(scores, axis=1, keepdims=True)
        expo = jnp.exp(scores - top)
        o_v[i] = contract(expo.astype(BF16), v, ((1,), (0,)))
        m_v[i] = jnp.broadcast_to(top, (lines, HD))
        l_v[i] = jnp.broadcast_to(jnp.sum(expo, axis=1, keepdims=True), (lines, HD))
        return carry

    done = [0]

    def some_cached(upto):
        upto = min(upto, packs)
        if upto > done[0]:
            lax.fori_loop(done[0], upto, cached, 0)
            done[0] = upto

    def reorder():
        lanes = [
            jnp.concatenate([hid_v[hh * nt + k] for k in range(nt)], axis=1) for hh in range(nh)
        ]
        natural = jnp.concatenate(lanes, axis=0)
        depth = blocks * sub
        lanes_at = min(256, depth)
        line_ = lax.broadcasted_iota(jnp.int32, (depth, lanes_at), 0)
        for n in range(0, depth, lanes_at):
            pick = jnp.where(line_ == target_v[:, n : n + lanes_at], 1.0, 0.0).astype(BF16)
            ordered_v[:, n : n + lanes_at] = contract(natural, pick, ((1,), (0,))).astype(BF16)

    core = lax.rem(t, 2)
    chip = t // 2
    sibling = t + 1 - 2 * core

    def pair_copy(c):
        own = pl.ds(c * band_chips, band_chips)
        return remote(give_v.at[own], take_v.at[own], pair_send.at[c], pair_recv.at[c], (f, sibling))

    def product(c):
        depth = 2 * ny * TILE
        acc = None
        for k in range(nz // 2):
            if c == 0:
                w = w_v[c][2 * k * ny : (2 * k + 2) * ny].reshape(depth, band_chips * 2 * HD)
            else:
                w = jnp.concatenate(
                    [w_v[c][yy * nz + zz] for zz in (2 * k, 2 * k + 1) for yy in range(ny)], axis=0
                )
            term = contract(ordered_v[:, k * depth : (k + 1) * depth], w, ((1,), (0,)))
            acc = term if acc is None else acc + term
        for j in range(band_chips):
            one = acc[:, 2 * j * HD : (2 * j + 1) * HD]
            two = acc[:, (2 * j + 1) * HD : (2 * j + 2) * HD]
            mine_v[c * band_chips + j] = jnp.where(core == 0, one, two)
            give_v[c * band_chips + j] = jnp.where(core == 0, two, one)
        start(pair_copy(c))

    def to_owner(c, dh):
        hh = lax.rem(h + dh, nh)
        return remote(
            out_v.at[c, pl.ds(pl.multiple_of(hh * total, 16), total)],
            part_in_v.at[h * chips + chip],
            p6_send.at[c, dh],
            p6_recv.at[dh * chips + lax.rem(c - chip + chips, chips)],
            at(z, y, hh, 2 * c + core),
        )

    def each_owner(c, act):
        for dh in range(nh):
            if dh:
                act(to_owner(c, dh))
            else:

                @pl.when(chip != c)
                def _():
                    act(to_owner(c, 0))

    def combine(band):
        pair_copy(band).wait_recv()
        for c in range(band * band_chips, (band + 1) * band_chips):
            both = mine_v[c] + take_v[c]
            mine_v[c] = both
            out_v[c] = both.astype(BF16)
            each_owner(c, lambda copy: copy.start())

    steps = max(ny, nz) // 2
    for c in range(bands):
        stage1_wait(c)
    for half in range(CUTS):
        stage2_send(0, half)
    for step in range(1, steps):
        for half in range(CUTS):
            some_cached(-(-packs * (CUTS * (step - 1) + half + 1) // (CUTS * (steps - 1))))
            stage2_wait(step - 1, half)
            stage2_send(step, half)
    some_cached(packs)
    hidden_wait()
    reorder()
    for half in range(CUTS):
        stage2_wait(steps - 1, half)
    for c in range(bands):
        product(c)
    for c in range(bands):
        combine(c)

    keys = mine_v[chip, pl.ds(pl.multiple_of(h * total, 16), total)]
    for dh in range(nh):
        for d in range(chips):
            if (dh, d) != (0, 0):
                source = lax.rem(h + nh - dh, nh) * chips + lax.rem(chip + chips - d, chips)
                into = part_in_v.at[source]
                remote(into, into, p6_send.at[0, 0], p6_recv.at[dh * chips + d], (f, sibling)).wait_recv()
                keys = keys + part_in_v[source].astype(F32)
    keys16 = keys.astype(BF16)
    keys32 = keys16.astype(F32)
    fresh_v[...] = keys32
    keys_ref[0] = keys32[:rows].astype(BF16)
    keys_ref[1] = keys32[rows:].astype(BF16)

    line2 = lax.broadcasted_iota(jnp.int32, (lines, 16), 0)
    place2 = lax.broadcasted_iota(jnp.int32, (lines, 16), 1)
    allowed = (lax.rem(line2, 8) == lax.rem(place2, 8)) & (place2 // 8 <= line2 // (heads * 8))

    def finish(i, carry):
        row = pl.multiple_of(i * 8, 8)
        late = pl.multiple_of(rows + i * 8, 8)
        nk = jnp.concatenate([fresh_v[pl.ds(row, 8)], fresh_v[pl.ds(late, 8)]], axis=0).astype(BF16)
        nv = jnp.concatenate([nval_v[pl.ds(row, 8)], nval_v[pl.ds(late, 8)]], axis=0).astype(BF16)
        scores = jnp.where(allowed, contract(q_v[i], nk, ((1,), (1,))) * factor, NEG)
        old = m_v[i]
        top = jnp.maximum(old, jnp.max(scores, axis=1, keepdims=True))
        keep = jnp.exp(old - top)
        expo = jnp.exp(scores - top[:, :16])
        weight = l_v[i] * keep + jnp.sum(expo, axis=1, keepdims=True)
        out = (o_v[i] * keep + contract(expo.astype(BF16), nv, ((1,), (0,)))) / weight
        for s in range(2):
            for g in range(heads):
                at_line = (s * heads + g) * 8
                result_v[s, pl.ds(row, 8), g * HD : (g + 1) * HD] = out[at_line : at_line + 8]
        return carry

    lax.fori_loop(0, packs, finish, 0)
    attended_ref[...] = result_v[...].astype(BF16)

    for copy in sent:
        copy.wait_send()
    for c in range(chips):
        each_owner(c, lambda copy: copy.wait_send())


def hand_over(attended_in, keys_in, attended_out, keys_out, attended_v, keys_v, in_sem, out_sem):
    half = attended_in.shape[2] // 2
    spans = [(s, slice(None), pl.ds(k * half, half)) for s in range(2) for k in range(2)]
    routes = [(keys_in, keys_v, keys_out)]
    routes += [(attended_in.at[span], attended_v.at[span], attended_out.at[span]) for span in spans]
    into = [pltpu.make_async_copy(r[0], r[1], in_sem.at[i]) for i, r in enumerate(routes)]
    out = [pltpu.make_async_copy(r[1], r[2], out_sem.at[i]) for i, r in enumerate(routes)]
    for copy in into:
        copy.start()
    for arrived, copy in zip(into, out):
        arrived.wait()
        copy.start()
    for copy in out:
        copy.wait()


def per_device(
    grid,
    nt,
    hidden,
    queries,
    cache_keys,
    cache_values,
    new_values,
    lengths,
    base_weight,
    delta_values,
    delta_scales,
    block_order,
):
    nz, ny, nh = grid
    blocks = nz * ny * nh
    rows = hidden.shape[1]
    blk = base_weight.shape[0] // blocks
    assert blk == nt * TILE and base_weight.shape[1] == HD
    chips = nt // 2
    total = 2 * rows
    assert nh == 2
    span = blocks // nt * TILE // nh
    width = nt * nh * span
    heads = queries.shape[2] // HD
    packs = rows // 8
    lines = 2 * heads * 8
    cap = cache_keys.shape[1]
    ring = max(ny, nz)
    xs = nh * nt - 1
    dma = pltpu.SemaphoreType.DMA
    smem = pltpu.SMEM
    scratch = [
        smem(block_order.shape, jnp.int32),
        smem(lengths.shape, jnp.int32),
        pltpu.VMEM((1, blocks * TILE // nh), jnp.int32),
        pltpu.VMEM((1, 1), BF16),
        pltpu.VMEM((blocks, blk, HD), BF16),
        pltpu.VMEM(delta_values.shape, BF16),
        pltpu.VMEM(new_values.shape, BF16),
        pltpu.VMEM((nt, 2 * TILE, HD), BF16),
        pltpu.VMEM(hidden.shape, BF16),
        pltpu.VMEM(queries.shape, BF16),
        pltpu.VMEM(cache_keys.shape, BF16),
        pltpu.VMEM(cache_values.shape, BF16),
        pltpu.VMEM((total, width), BF16),
        pltpu.VMEM((width, nh * span), BF16),
        pltpu.VMEM((nh * nt, total, span), BF16),
        pltpu.VMEM((nh * nt, total, span), BF16),
        pltpu.VMEM((nh * nt, 2 * TILE, HD), BF16),
        pltpu.VMEM((nh, TILE, nt * HD), BF16),
        pltpu.VMEM(queries.shape, F32),
        *[pltpu.VMEM((blocks // nh, TILE, nt * HD // 2), BF16) for _ in range(2)],
        pltpu.VMEM((nh * total, blocks * TILE // nh), BF16),
        pltpu.VMEM((chips, nh * total, HD), F32),
        pltpu.VMEM((chips, nh * total, HD), F32),
        pltpu.VMEM((chips, nh * total, HD), F32),
        pltpu.VMEM((chips, nh * total, HD), BF16),
        pltpu.VMEM((nh * chips, total, HD), BF16),
        pltpu.VMEM((total, HD), F32),
        pltpu.VMEM((total, HD), F32),
        pltpu.VMEM((packs, lines, HD), BF16),
        pltpu.VMEM((packs, lines, HD), F32),
        pltpu.VMEM((packs, lines, HD), F32),
        pltpu.VMEM((packs, lines, HD), F32),
        pltpu.VMEM((lines, 8 * cap), F32),
        pltpu.VMEM(queries.shape, F32),
        dma((10,)),
        dma((xs,)),
        dma((xs,)),
        dma,
        dma,
        dma((xs,)),
        dma((xs,)),
        dma((2, ring)),
        dma((2, ring)),
        dma((2, 2, ring // 2, CUTS)),
        dma((2, 2, ring // 2, CUTS)),
        dma((2,)),
        dma((2,)),
        dma((chips, nh)),
        dma((nh * chips,)),
    ]
    vmem = pl.BlockSpec(memory_space=pltpu.VMEM)
    hbm = pl.BlockSpec(memory_space=pltpu.HBM)
    results = tuple(
        pl.pallas_call(
            functools.partial(kernel, (nz, ny, nh, nt, rows)),
            out_shape=(
                jax.ShapeDtypeStruct(queries.shape, BF16),
                jax.ShapeDtypeStruct((2, rows, HD), BF16),
            ),
            in_specs=[hbm] * 10,
            out_specs=(vmem, vmem),
            scratch_shapes=scratch,
            compiler_params=pltpu.CompilerParams(
                collective_id=0, has_side_effects=True, vmem_limit_bytes=63 * 2**20
            ),
            name="refresh_project_attend",
        )(
            block_order,
            lengths,
            delta_scales,
            base_weight.reshape(blocks, blk, HD),
            delta_values,
            hidden,
            queries,
            cache_keys,
            cache_values,
            new_values,
        )
    )
    return pl.pallas_call(
        hand_over,
        out_shape=tuple(jax.ShapeDtypeStruct(r.shape, r.dtype) for r in results),
        in_specs=[hbm] * 2,
        out_specs=(hbm, hbm),
        scratch_shapes=[pltpu.VMEM(r.shape, r.dtype) for r in results] + [dma((5,)), dma((5,))],
        compiler_params=pltpu.CompilerParams(vmem_limit_bytes=63 * 2**20),
        name="hand_over",
    )(*results)


def solution(mesh, grid=None):
    grid = grid or GRID[mesh.shape["fsdp"]]
    in_specs = (
        P(None, "fsdp", "tp"),
        P(None, "fsdp", "tp"),
        P("fsdp", None, "tp"),
        P("fsdp", None, "tp"),
        P(None, "fsdp", "tp"),
        P("fsdp"),
        P(None, "tp"),
        P(("fsdp", "tp"), None),
        P("fsdp", "tp"),
        P(),
    )
    out_specs = (P(None, "fsdp", "tp"), P(None, "fsdp", "tp"))
    return jax.shard_map(
        functools.partial(per_device, grid, mesh.shape["tp"]),
        mesh=mesh,
        in_specs=in_specs,
        out_specs=out_specs,
        check_vma=False,
    )
```

```python
import functools
import math

import jax
import jax.numpy as jnp
from jax import lax
from jax.experimental import pallas as pl
from jax.experimental.pallas import tpu as pltpu
from jax.sharding import PartitionSpec as P

HD = 128
TILE = 16
MESH = pl.DeviceIdType.MESH
F32 = jnp.float32
BF16 = jnp.bfloat16
GRID = {128: (8, 8, 2)}
NEG = -1e30
CUTS = 4


def contract(a, b, dims):
    return lax.dot_general(a, b, (dims, ((), ())), preferred_element_type=F32)


def kernel(
    dims,
    order_hbm,
    lengths_hbm,
    scale_hbm,
    base_hbm,
    delta_hbm,
    hidden_hbm,
    queries_hbm,
    ckeys_hbm,
    cvals_hbm,
    nvals_hbm,
    attended_ref,
    keys_ref,
    order_ref,
    lengths_ref,
    target_v,
    scale_v,
    base_v,
    delta_ref,
    nvals_ref,
    parcel_ref,
    hidden_v,
    queries_v,
    ckeys_v,
    cvals_v,
    hidden_all_v,
    pick_v,
    regroup_v,
    hid_v,
    parcels_v,
    deltas_v,
    wide_v,
    *rest,
):
    nz, ny, nh, nt, rows = dims
    blocks = nz * ny * nh
    local_blocks = blocks // nt
    chips = nt // 2
    total = 2 * rows
    sub = TILE // nh
    span = local_blocks * sub
    width = nt * nh * span
    heads = attended_ref.shape[2] // HD
    packs = rows // 8
    lines = 2 * heads * 8
    cap = ckeys_v.shape[1]
    keys8 = 8 * cap
    factor = 1.0 / math.sqrt(HD)

    bands = 2
    band_chips = chips // bands
    w_v = rest[:bands]
    (
        ordered_v,
        mine_v,
        give_v,
        take_v,
        out_v,
        part_in_v,
        fresh_v,
        nval_v,
        q_v,
        o_v,
        m_v,
        l_v,
        mask_v,
        result_v,
        load_sem,
        p0_send,
        p0_recv,
        delta_send,
        delta_recv,
        hid_send,
        hid_recv,
        s1_send,
        s1_recv,
        s2_send,
        s2_recv,
        pair_send,
        pair_recv,
        p6_send,
        p6_recv,
    ) = rest[bands:]

    f = lax.axis_index("fsdp")
    t = lax.axis_index("tp")
    h = lax.rem(f, nh)
    y = lax.rem(f // nh, ny)
    z = f // (nh * ny)

    def at(zz, yy, hh, tt):
        return ((zz * ny + yy) * nh + hh, tt)

    def y_peer(step):
        return at(z, lax.rem(y + step + ny, ny), h, t)

    def z_peer(step):
        return at(lax.rem(z + step + nz, nz), y, h, t)

    def x_peer(dh, d):
        return at(z, y, lax.rem(h + dh, nh), lax.rem(t + d, nt))

    x_peers = [(dh, d) for dh in range(nh) for d in range(nt) if (dh, d) != (0, 0)]

    loads = [
        pltpu.make_async_copy(src, dst, load_sem.at[i])
        for i, (src, dst) in enumerate(
            (
                (order_hbm, order_ref),
                (scale_hbm, scale_v),
                (base_hbm, base_v),
                (delta_hbm, delta_ref),
                (hidden_hbm, hidden_v),
                (lengths_hbm, lengths_ref),
                (queries_hbm, queries_v),
                (ckeys_hbm, ckeys_v),
                (cvals_hbm, cvals_v),
                (nvals_hbm, nvals_ref),
            )
        )
    ]
    for load in loads[:4]:
        load.start()

    barrier = pltpu.get_barrier_semaphore()
    count = 0
    for peer in (
        [x_peer(*p) for p in x_peers]
        + [y_peer(s) for s in range(1, ny)]
        + [z_peer(s) for s in range(1, nz)]
    ):
        pl.semaphore_signal(barrier, inc=1, device_id=peer, device_id_type=MESH)
        count += 1
    for load in loads[:4]:
        load.wait()
    for load in loads[4:]:
        load.start()
    parcel_ref[:, :TILE] = base_v[order_ref[f]].reshape(nt, TILE, HD)
    parcel_ref[:, TILE:] = jnp.broadcast_to(scale_v[...].reshape(1, 1, 1), (nt, TILE, HD))
    pl.semaphore_wait(barrier, count)

    def remote(src, dst, send, recv, peer):
        return pltpu.make_async_remote_copy(
            src_ref=src, dst_ref=dst, send_sem=send, recv_sem=recv, device_id=peer, device_id_type=MESH
        )

    sent = []

    def start(copy):
        copy.start()
        sent.append(copy)

    for i, (dh, d) in enumerate(x_peers):
        start(
            remote(
                parcel_ref.at[lax.rem(t + d, nt)],
                parcels_v.at[h * nt + t],
                p0_send.at[i],
                p0_recv.at[i],
                x_peer(dh, d),
            )
        )
    if nh > 1:
        start(remote(delta_ref, deltas_v.at[h], delta_send, delta_recv, x_peer(1, 0)))
    parcels_v[h * nt + t] = parcel_ref[t]
    deltas_v[h] = delta_ref[...]

    def hidden_wait():
        for i, (dh, d) in enumerate(x_peers):
            source = lax.rem(h + nh - dh, nh) * nt + lax.rem(t + nt - d, nt)
            remote(regroup_v.at[0], hid_v.at[source], hid_send.at[i], hid_recv.at[i], x_peer(dh, d)).wait_recv()

    for i, (dh, d) in enumerate(x_peers):
        source = lax.rem(h + nh - dh, nh) * nt + lax.rem(t + nt - d, nt)
        remote(parcel_ref.at[0], parcels_v.at[source], p0_send.at[i], p0_recv.at[i], x_peer(dh, d)).wait_recv()
    if nh > 1:
        remote(delta_ref, deltas_v.at[1 - h], delta_send, delta_recv, x_peer(1, 0)).wait_recv()

    def axes(c):
        if c == 0:
            return (y, ny, y_peer), (z, nz, z_peer)
        return (z, nz, z_peer), (y, ny, y_peer)

    def half_of(rows16):
        out = rows16[:sub]
        for hh in range(1, nh):
            out = jnp.where(h == hh, rows16[hh * sub : (hh + 1) * sub], out)
        return out

    for c in range(bands):
        (a, na, _), (b, nb, _) = axes(c)
        cols = []
        for col in range(c * nt // bands, (c + 1) * nt // bands):
            parts = []
            for hh in range(nh):
                parcel = parcels_v[hh * nt + col].astype(F32)
                update = deltas_v[hh, :, col * HD : (col + 1) * HD].astype(F32)
                scaled = (half_of(update) * parcel[TILE : TILE + sub]).astype(BF16).astype(F32)
                parts.append(half_of(parcel[:TILE]) + scaled)
            cols.append(jnp.concatenate(parts, axis=0))
        w_v[c][b * na + a] = jnp.concatenate(cols, axis=1).astype(BF16)

    def stage1_piece(c, source_a):
        (a, na, _), (b, nb, _) = axes(c)
        return w_v[c].at[pl.ds(b * na + source_a, 1)]

    def stage1_send(c):
        (a, na, peer), _ = axes(c)
        for s in range(1, na):
            start(remote(stage1_piece(c, a), stage1_piece(c, a), s1_send.at[c, s], s1_recv.at[c, s], peer(s)))

    def stage1_wait(c):
        (a, na, peer), _ = axes(c)
        for s in range(1, na):
            piece = stage1_piece(c, lax.rem(a + na - s, na))
            remote(piece, piece, s1_send.at[c, s], s1_recv.at[c, s], peer(s)).wait_recv()

    def unit(c, which, half):
        (a, na, _), (b, nb, _) = axes(c)
        size = na // CUTS
        start_row = lax.rem(b + which + 2 * nb, nb) * na + half * size
        return w_v[c].at[pl.ds(start_row, size)]

    def hops(c, way, half):
        nb = axes(c)[1][1]
        return nb // 2 if (half < CUTS // 2) == (way == 0) else nb - 1 - nb // 2

    def stage2_each(step, half, ahead, act):
        for c in range(bands):
            peer = axes(c)[1][2]
            for way, sign in enumerate((1, -1)):
                if step < hops(c, way, half):
                    piece = unit(c, -sign * (step + ahead), half)
                    act(
                        remote(
                            piece, piece, s2_send.at[c, way, step, half], s2_recv.at[c, way, step, half], peer(sign)
                        )
                    )

    def stage2_send(step, half):
        stage2_each(step, half, 0, start)

    def stage2_wait(step, half):
        stage2_each(step, half, 1, lambda copy: copy.wait_recv())

    for c in range(bands):
        stage1_send(c)

    lane_k = lax.broadcasted_iota(jnp.int32, (width, nh * span), 0)
    lane_l = lax.broadcasted_iota(jnp.int32, (width, nh * span), 1)
    target = lax.rem(lane_k, TILE) // sub * span + lane_k // (nt * TILE) * sub + lax.rem(lane_k, sub)
    pick_v[...] = jnp.where(target == lane_l, 1.0, 0.0).astype(BF16)
    loads[4].wait()
    hidden_all_v[...] = jnp.concatenate([hidden_v[0].astype(F32), hidden_v[1].astype(F32)], axis=0).astype(BF16)
    group_of = lax.rem(lax.broadcasted_iota(jnp.int32, (1, width), 1) // TILE, nt)

    def regroup(g, carry):
        chosen = hidden_all_v[...] * jnp.where(group_of == g, 1.0, 0.0).astype(BF16)
        out = contract(chosen, pick_v[...], ((1,), (0,))).astype(BF16)
        for hh in range(nh):
            regroup_v[hh * nt + g] = out[:, hh * span : (hh + 1) * span]
        return carry

    lax.fori_loop(0, nt, regroup, 0)
    for i, (dh, d) in enumerate(x_peers):
        start(
            remote(
                regroup_v.at[lax.rem(h + dh, nh) * nt + lax.rem(t + d, nt)],
                hid_v.at[h * nt + t],
                hid_send.at[i],
                hid_recv.at[i],
                x_peer(dh, d),
            )
        )
    hid_v[h * nt + t] = regroup_v[h * nt + t]

    for load in loads[5:]:
        load.wait()
    wide_v[...] = queries_v[...].astype(F32)
    line = lax.broadcasted_iota(jnp.int32, (lines, keys8), 0)
    place = lax.broadcasted_iota(jnp.int32, (lines, keys8), 1)
    mask_v[...] = jnp.where(lax.rem(line, 8) == place // cap, 0.0, NEG)
    nval_v[...] = jnp.concatenate([nvals_ref[0].astype(F32), nvals_ref[1].astype(F32)], axis=0)

    place_l = lax.broadcasted_iota(jnp.int32, (1, blocks * sub), 1)

    def aim(p, row):
        return jnp.where(place_l // sub == p, order_ref[p] * sub, row)

    aimed = lax.fori_loop(0, blocks, aim, jnp.zeros((1, blocks * sub), jnp.int32))
    target_v[...] = aimed + lax.rem(place_l, sub)

    def cached(i, carry):
        row = pl.multiple_of(i * 8, 8)
        parts = [
            wide_v[s, pl.ds(row, 8), g * HD : (g + 1) * HD] for s in range(2) for g in range(heads)
        ]
        q = jnp.concatenate(parts, axis=0).astype(BF16)
        q_v[i] = q
        k = ckeys_v[pl.ds(row, 8)].reshape(keys8, HD)
        v = cvals_v[pl.ds(row, 8)].reshape(keys8, HD)
        slot = lax.broadcasted_iota(jnp.int32, (1, keys8), 1)
        limit = jnp.zeros((1, keys8), jnp.int32)
        for r in range(8):
            limit = jnp.where(slot // cap == r, lengths_ref[row + r], limit)
        open_slot = lax.rem(slot, cap) < limit
        scores = contract(q, k, ((1,), (1,))) * factor
        scores = jnp.where(open_slot, scores + mask_v[...], NEG)
        top = jnp.max(scores, axis=1, keepdims=True)
        expo = jnp.exp(scores - top)
        o_v[i] = contract(expo.astype(BF16), v, ((1,), (0,)))
        m_v[i] = jnp.broadcast_to(top, (lines, HD))
        l_v[i] = jnp.broadcast_to(jnp.sum(expo, axis=1, keepdims=True), (lines, HD))
        return carry

    done = [0]

    def some_cached(upto):
        upto = min(upto, packs)
        if upto > done[0]:
            lax.fori_loop(done[0], upto, cached, 0)
            done[0] = upto

    def reorder():
        lanes = [
            jnp.concatenate([hid_v[hh * nt + k] for k in range(nt)], axis=1) for hh in range(nh)
        ]
        natural = jnp.concatenate(lanes, axis=0)
        depth = blocks * sub
        lanes_at = min(256, depth)
        line_ = lax.broadcasted_iota(jnp.int32, (depth, lanes_at), 0)
        for n in range(0, depth, lanes_at):
            pick = jnp.where(line_ == target_v[:, n : n + lanes_at], 1.0, 0.0).astype(BF16)
            ordered_v[:, n : n + lanes_at] = contract(natural, pick, ((1,), (0,))).astype(BF16)

    core = lax.rem(t, 2)
    chip = t // 2
    sibling = t + 1 - 2 * core

    def pair_copy(c):
        own = pl.ds(c * band_chips, band_chips)
        return remote(give_v.at[own], take_v.at[own], pair_send.at[c], pair_recv.at[c], (f, sibling))

    def product(c):
        depth = 2 * ny * TILE
        acc = None
        for k in range(nz // 2):
            if c == 0:
                w = w_v[c][2 * k * ny : (2 * k + 2) * ny].reshape(depth, band_chips * 2 * HD)
            else:
                w = jnp.concatenate(
                    [w_v[c][yy * nz + zz] for zz in (2 * k, 2 * k + 1) for yy in range(ny)], axis=0
                )
            term = contract(ordered_v[:, k * depth : (k + 1) * depth], w, ((1,), (0,)))
            acc = term if acc is None else acc + term
        for j in range(band_chips):
            one = acc[:, 2 * j * HD : (2 * j + 1) * HD]
            two = acc[:, (2 * j + 1) * HD : (2 * j + 2) * HD]
            mine_v[c * band_chips + j] = jnp.where(core == 0, one, two)
            give_v[c * band_chips + j] = jnp.where(core == 0, two, one)
        start(pair_copy(c))

    def to_owner(c, dh):
        hh = lax.rem(h + dh, nh)
        return remote(
            out_v.at[c, pl.ds(pl.multiple_of(hh * total, 16), total)],
            part_in_v.at[h * chips + chip],
            p6_send.at[c, dh],
            p6_recv.at[dh * chips + lax.rem(c - chip + chips, chips)],
            at(z, y, hh, 2 * c + core),
        )

    def each_owner(c, act):
        for dh in range(nh):
            if dh:
                act(to_owner(c, dh))
            else:

                @pl.when(chip != c)
                def _():
                    act(to_owner(c, 0))

    def combine(band):
        pair_copy(band).wait_recv()
        for c in range(band * band_chips, (band + 1) * band_chips):
            both = mine_v[c] + take_v[c]
            mine_v[c] = both
            out_v[c] = both.astype(BF16)
            each_owner(c, lambda copy: copy.start())

    steps = max(ny, nz) // 2
    for c in range(bands):
        stage1_wait(c)
    for half in range(CUTS):
        stage2_send(0, half)
    for step in range(1, steps):
        for half in range(CUTS):
            some_cached(-(-packs * (CUTS * (step - 1) + half + 1) // (CUTS * (steps - 1))))
            stage2_wait(step - 1, half)
            stage2_send(step, half)
    some_cached(packs)
    hidden_wait()
    reorder()
    for half in range(CUTS):
        stage2_wait(steps - 1, half)
    for c in range(bands):
        product(c)
    for c in range(bands):
        combine(c)

    keys = mine_v[chip, pl.ds(pl.multiple_of(h * total, 16), total)]
    for dh in range(nh):
        for d in range(chips):
            if (dh, d) != (0, 0):
                source = lax.rem(h + nh - dh, nh) * chips + lax.rem(chip + chips - d, chips)
                into = part_in_v.at[source]
                remote(into, into, p6_send.at[0, 0], p6_recv.at[dh * chips + d], (f, sibling)).wait_recv()
                keys = keys + part_in_v[source].astype(F32)
    keys16 = keys.astype(BF16)
    keys32 = keys16.astype(F32)
    fresh_v[...] = keys32
    keys_ref[0] = keys32[:rows].astype(BF16)
    keys_ref[1] = keys32[rows:].astype(BF16)

    line2 = lax.broadcasted_iota(jnp.int32, (lines, 16), 0)
    place2 = lax.broadcasted_iota(jnp.int32, (lines, 16), 1)
    allowed = (lax.rem(line2, 8) == lax.rem(place2, 8)) & (place2 // 8 <= line2 // (heads * 8))

    def finish(i, carry):
        row = pl.multiple_of(i * 8, 8)
        late = pl.multiple_of(rows + i * 8, 8)
        nk = jnp.concatenate([fresh_v[pl.ds(row, 8)], fresh_v[pl.ds(late, 8)]], axis=0).astype(BF16)
        nv = jnp.concatenate([nval_v[pl.ds(row, 8)], nval_v[pl.ds(late, 8)]], axis=0).astype(BF16)
        scores = jnp.where(allowed, contract(q_v[i], nk, ((1,), (1,))) * factor, NEG)
        old = m_v[i]
        top = jnp.maximum(old, jnp.max(scores, axis=1, keepdims=True))
        keep = jnp.exp(old - top)
        expo = jnp.exp(scores - top[:, :16])
        weight = l_v[i] * keep + jnp.sum(expo, axis=1, keepdims=True)
        out = (o_v[i] * keep + contract(expo.astype(BF16), nv, ((1,), (0,)))) / weight
        for s in range(2):
            for g in range(heads):
                at_line = (s * heads + g) * 8
                result_v[s, pl.ds(row, 8), g * HD : (g + 1) * HD] = out[at_line : at_line + 8]
        return carry

    lax.fori_loop(0, packs, finish, 0, unroll=3)
    attended_ref[...] = result_v[...].astype(BF16)

    for copy in sent:
        copy.wait_send()
    for c in range(chips):
        each_owner(c, lambda copy: copy.wait_send())


def hand_over(attended_in, keys_in, attended_out, keys_out, attended_v, keys_v, in_sem, out_sem):
    half = attended_in.shape[2] // 2
    spans = [(s, slice(None), pl.ds(k * half, half)) for s in range(2) for k in range(2)]
    routes = [(keys_in, keys_v, keys_out)]
    routes += [(attended_in.at[span], attended_v.at[span], attended_out.at[span]) for span in spans]
    into = [pltpu.make_async_copy(r[0], r[1], in_sem.at[i]) for i, r in enumerate(routes)]
    out = [pltpu.make_async_copy(r[1], r[2], out_sem.at[i]) for i, r in enumerate(routes)]
    for copy in into:
        copy.start()
    for arrived, copy in zip(into, out):
        arrived.wait()
        copy.start()
    for copy in out:
        copy.wait()


def per_device(
    grid,
    nt,
    hidden,
    queries,
    cache_keys,
    cache_values,
    new_values,
    lengths,
    base_weight,
    delta_values,
    delta_scales,
    block_order,
):
    nz, ny, nh = grid
    blocks = nz * ny * nh
    rows = hidden.shape[1]
    blk = base_weight.shape[0] // blocks
    assert blk == nt * TILE and base_weight.shape[1] == HD
    chips = nt // 2
    total = 2 * rows
    assert nh == 2
    span = blocks // nt * TILE // nh
    width = nt * nh * span
    heads = queries.shape[2] // HD
    packs = rows // 8
    lines = 2 * heads * 8
    cap = cache_keys.shape[1]
    ring = max(ny, nz)
    xs = nh * nt - 1
    dma = pltpu.SemaphoreType.DMA
    smem = pltpu.SMEM
    scratch = [
        smem(block_order.shape, jnp.int32),
        smem(lengths.shape, jnp.int32),
        pltpu.VMEM((1, blocks * TILE // nh), jnp.int32),
        pltpu.VMEM((1, 1), BF16),
        pltpu.VMEM((blocks, blk, HD), BF16),
        pltpu.VMEM(delta_values.shape, BF16),
        pltpu.VMEM(new_values.shape, BF16),
        pltpu.VMEM((nt, 2 * TILE, HD), BF16),
        pltpu.VMEM(hidden.shape, BF16),
        pltpu.VMEM(queries.shape, BF16),
        pltpu.VMEM(cache_keys.shape, BF16),
        pltpu.VMEM(cache_values.shape, BF16),
        pltpu.VMEM((total, width), BF16),
        pltpu.VMEM((width, nh * span), BF16),
        pltpu.VMEM((nh * nt, total, span), BF16),
        pltpu.VMEM((nh * nt, total, span), BF16),
        pltpu.VMEM((nh * nt, 2 * TILE, HD), BF16),
        pltpu.VMEM((nh, TILE, nt * HD), BF16),
        pltpu.VMEM(queries.shape, F32),
        *[pltpu.VMEM((blocks // nh, TILE, nt * HD // 2), BF16) for _ in range(2)],
        pltpu.VMEM((nh * total, blocks * TILE // nh), BF16),
        pltpu.VMEM((chips, nh * total, HD), F32),
        pltpu.VMEM((chips, nh * total, HD), F32),
        pltpu.VMEM((chips, nh * total, HD), F32),
        pltpu.VMEM((chips, nh * total, HD), BF16),
        pltpu.VMEM((nh * chips, total, HD), BF16),
        pltpu.VMEM((total, HD), F32),
        pltpu.VMEM((total, HD), F32),
        pltpu.VMEM((packs, lines, HD), BF16),
        pltpu.VMEM((packs, lines, HD), F32),
        pltpu.VMEM((packs, lines, HD), F32),
        pltpu.VMEM((packs, lines, HD), F32),
        pltpu.VMEM((lines, 8 * cap), F32),
        pltpu.VMEM(queries.shape, F32),
        dma((10,)),
        dma((xs,)),
        dma((xs,)),
        dma,
        dma,
        dma((xs,)),
        dma((xs,)),
        dma((2, ring)),
        dma((2, ring)),
        dma((2, 2, ring // 2, CUTS)),
        dma((2, 2, ring // 2, CUTS)),
        dma((2,)),
        dma((2,)),
        dma((chips, nh)),
        dma((nh * chips,)),
    ]
    vmem = pl.BlockSpec(memory_space=pltpu.VMEM)
    hbm = pl.BlockSpec(memory_space=pltpu.HBM)
    results = tuple(
        pl.pallas_call(
            functools.partial(kernel, (nz, ny, nh, nt, rows)),
            out_shape=(
                jax.ShapeDtypeStruct(queries.shape, BF16),
                jax.ShapeDtypeStruct((2, rows, HD), BF16),
            ),
            in_specs=[hbm] * 10,
            out_specs=(vmem, vmem),
            scratch_shapes=scratch,
            compiler_params=pltpu.CompilerParams(
                collective_id=0, has_side_effects=True, vmem_limit_bytes=63 * 2**20
            ),
            name="refresh_project_attend",
        )(
            block_order,
            lengths,
            delta_scales,
            base_weight.reshape(blocks, blk, HD),
            delta_values,
            hidden,
            queries,
            cache_keys,
            cache_values,
            new_values,
        )
    )
    return pl.pallas_call(
        hand_over,
        out_shape=tuple(jax.ShapeDtypeStruct(r.shape, r.dtype) for r in results),
        in_specs=[hbm] * 2,
        out_specs=(hbm, hbm),
        scratch_shapes=[pltpu.VMEM(r.shape, r.dtype) for r in results] + [dma((5,)), dma((5,))],
        compiler_params=pltpu.CompilerParams(vmem_limit_bytes=63 * 2**20),
        name="hand_over",
    )(*results)


def solution(mesh, grid=None):
    grid = grid or GRID[mesh.shape["fsdp"]]
    in_specs = (
        P(None, "fsdp", "tp"),
        P(None, "fsdp", "tp"),
        P("fsdp", None, "tp"),
        P("fsdp", None, "tp"),
        P(None, "fsdp", "tp"),
        P("fsdp"),
        P(None, "tp"),
        P(("fsdp", "tp"), None),
        P("fsdp", "tp"),
        P(),
    )
    out_specs = (P(None, "fsdp", "tp"), P(None, "fsdp", "tp"))
    return jax.shard_map(
        functools.partial(per_device, grid, mesh.shape["tp"]),
        mesh=mesh,
        in_specs=in_specs,
        out_specs=out_specs,
        check_vma=False,
    )
```
